32 devices in a mesh: groups: 2 (over x), dp: 2 (over core), expert: 8 (over z, y).
Axes of the slice: x: 2, y: 2, z: 4, core: 2. Of those that a mesh axis runs over, the one named last changes fastest.
Arguments:
- tokens: bfloat16 [4096, 3584], P(('groups', 'dp', 'expert')), parts along dimension 0, may hold values from -6 to 6
- scores: float32 [4096, 8], P(('groups', 'dp', 'expert')), parts along dimension 0, may hold values from -8 to 8
- expert_ids: int32 [4096, 2], P(('groups', 'dp', 'expert')), parts along dimension 0, may hold values from 0 to 7, all different within a row; in each aligned block of 128 rows (0 to 127, 128 to 255, ...) at most 80 rows name the same one
- w_gate: bfloat16 [8, 3584, 1024], P('expert', None, 'dp'), may hold values from -0.09375 to 0.09375
- w_up: bfloat16 [8, 3584, 1024], P('expert', None, 'dp'), may hold values from -0.09375 to 0.09375
- w_down: bfloat16 [8, 1024, 3584], P('expert', 'dp'), may hold values from -0.1875 to 0.1875
Outputs:
- mixed: bfloat16 [4096, 3584], P(('groups', 'dp', 'expert')), parts along dimension 0
The draws below stay inside these ranges and needn't reach their ends.
There are 2 independent parts, one for each index of `groups`. The reference program is written for one: setup_inputs(seed, part) draws one part's arguments, and reference() takes and returns one part's arrays. A program takes and returns all parts, laid end to end along the dimension named above; an argument that names none is the same for every part. Nothing has to cross between parts.
Inputs may be any that keep to these rules, and one draw needn't show every extreme that they name: `expert_ids`: the 2048 rows fall into aligned blocks of 128 rows, the rows of one device. Each row names 2 different experts. In no block is an expert named by more than 80 rows, and in every draw some block names some expert exactly 80 times.
All inputs are finite; a program needn't handle non-finite values.
Results may differ from the reference program's by a relative error of at most 0.0059.
Values may be sent and summed in bfloat16 or wider, within the bound.
No kernel may reach another device: no remote copies, remote signals or barrier semaphores. Data moves between devices by JAX's collectives and lax.ppermute only.
A program may use at most 128 MiB of HBM per device.

```python
import math
import jax
import jax.numpy as jnp
import numpy as np
from jax import lax

D = 3584
FF = 1024
TOPK = 2
TOK_DEV = 128
EXPERTS = 8
CAP = 80
TOKENS = 2048
N_DP = 2
N_EXPERT = 8


def shard_levels(rng, extent, pieces, smallest, largest):
    gain = 1.0
    for position, blocks in pieces:
        steps = jax.random.uniform(jax.random.fold_in(jax.random.fold_in(rng, 6), position), (blocks,), jnp.float32, smallest / len(pieces), largest / len(pieces))
        gain = gain * jnp.repeat(jnp.exp(steps), extent[position] // blocks).reshape((-1,) + (1,) * (len(extent) - 1 - position))
    return gain


def deal_out(own_key, own, number, rows, number_of, top, most, skew):
    sequence = jax.random.permutation(own_key, number_of)
    heavy_load, common = load_shares(number_of, rows * top, most, skew, True), load_shares(number_of, rows * top, most, skew, False)
    places = jnp.arange(number_of)

    def named(sizes, rotation):
        used = int((sizes > 0).sum())
        fixed = max(1, used // 4)
        passed = fixed + (places - fixed + rotation * (used - fixed)) % max(1, number_of - fixed)
        return jnp.zeros((number_of,), jnp.int32).at[sequence[jnp.where(places < fixed, places, passed)]].set(jnp.asarray(sizes, jnp.int32))

    sizes = jnp.where(number % 4 == 0, named(heavy_load, number // 4), named(common, number - number // 4 - 1))
    mixed = jax.random.permutation(jax.random.fold_in(own, 3), number_of)
    donor, taker = mixed[0:number_of // 2 * 2:2], mixed[1:number_of // 2 * 2:2]
    room = jnp.minimum(sizes[donor] - 1, most - sizes[taker]) // 2
    room = jnp.where((donor == sequence[0]) | (taker == sequence[0]) | (sizes[taker] == 0), 0, jnp.maximum(room, 0))
    passed = jax.random.randint(jax.random.fold_in(own, 4), (number_of // 2,), 0, 1 << 20) % (room + 1)
    sizes = sizes.at[donor].add(-passed).at[taker].add(passed)
    members = jnp.searchsorted(jnp.cumsum(sizes), jnp.arange(rows * top), side="right").astype(jnp.int32)
    table = members.reshape(top, rows).T
    table = table[jax.random.permutation(jax.random.fold_in(own, 1), rows)]
    rotation = jax.random.randint(jax.random.fold_in(own, 2), (rows, 1), 0, top)
    return jnp.take_along_axis(table, (jnp.arange(top)[None, :] + rotation) % top, axis=1)


def load_shares(count, total, most, skew, full):
    weights = [(1 << 20) // math.isqrt(rank ** skew) + 1 for rank in range(1, count + 1)]
    largest = most if full else min(most, max(-(-total // count), total * weights[0] // sum(weights)))
    least = 1 if total - largest >= count - 1 else 0
    holding, surplus = [largest] + [least] * (count - 1), total - largest - least * (count - 1)
    while surplus > 0:
        candidates = [i for i in range(1, count) if holding[i] < largest] or [i for i in range(1, count) if holding[i] < most]
        pool, left = sum([weights[i] for i in candidates]), surplus
        for i in candidates:
            extra = min(most - holding[i], max(1, left * weights[i] // pool), surplus)
            holding[i] = holding[i] + extra
            surplus = surplus - extra
    return np.array(holding)


def bell_draw(stream_key, shape, width, reach, pieces=(), kind=jnp.bfloat16):
    loudness = shard_levels(stream_key, shape, pieces, -0.22, 0.18) if pieces else 1.0
    drawn = jax.random.normal(stream_key, shape, jnp.float32) * width * loudness
    return jnp.minimum(jnp.maximum(drawn, -reach), reach).astype(kind)


def setup_inputs(seed: int = 0, part: int = 0) -> dict:
    key_of = jax.random.split(jax.random.key(seed), 7)
    part_keys = jax.random.split(jax.random.fold_in(key_of[6], part), 7)
    tokens = bell_draw(part_keys[0], (TOKENS, D), 1.0, 6.0, ((0, 16),))
    scores = bell_draw(part_keys[1], (TOKENS, EXPERTS), 1.5, 8.0, ((0, 16),), jnp.float32)
    expert_ids_keys = jax.random.split(jax.random.fold_in(part_keys[2], 1), TOKENS // TOK_DEV)
    expert_ids_turns = jax.random.permutation(jax.random.fold_in(part_keys[2], 3), TOKENS // TOK_DEV)
    expert_ids = jax.vmap(lambda own, number: deal_out(jax.random.fold_in(part_keys[2], 2), own, number, TOK_DEV, EXPERTS, TOPK, CAP, 2))(expert_ids_keys, expert_ids_turns).reshape((TOKENS, TOPK))
    w_gate = bell_draw(key_of[3], (EXPERTS, D, FF), D ** -0.5, 0.09375, ((0, 8), (2, 2)))
    w_up = bell_draw(key_of[4], (EXPERTS, D, FF), D ** -0.5, 0.09375, ((0, 8), (2, 2)))
    w_down = bell_draw(key_of[5], (EXPERTS, FF, D), FF ** -0.5, 0.1875, ((0, 8), (1, 2)))
    return dict(tokens=tokens, scores=scores, expert_ids=expert_ids, w_gate=w_gate, w_up=w_up, w_down=w_down)


def expert_rows(rows, gate_part, up_part, down_part):
    gate = jnp.dot(rows, gate_part, preferred_element_type=jnp.float32)
    up_value = jnp.dot(rows, up_part, preferred_element_type=jnp.float32)
    hidden = (jax.nn.silu(gate) * up_value).astype(jnp.bfloat16)
    return jnp.dot(hidden, down_part, preferred_element_type=jnp.float32).astype(jnp.bfloat16)


def reference(tokens, scores, expert_ids, w_gate, w_up, w_down):
    count = expert_ids.shape[0] * expert_ids.shape[1]
    flat_ids = expert_ids.reshape(-1)
    chosen = jax.nn.sigmoid(jnp.take_along_axis(scores, expert_ids, axis=1))
    weight = chosen / jnp.sum(chosen, axis=1, keepdims=True)
    flat_weight = weight.reshape(-1)
    limit = min(TOKENS, N_DP * N_EXPERT * CAP)
    order_keys = jnp.arange(count, dtype=jnp.int32)

    def step(total, packed):
        index, gate_part, up_part, down_part = packed
        member = flat_ids == index
        keys = jnp.where(member, order_keys, order_keys + count)
        picked = jnp.argsort(keys)[:limit].astype(jnp.int32)
        valid = member[picked]
        owner = (picked // TOPK).astype(jnp.int32)
        values = expert_rows(tokens[owner], gate_part, up_part, down_part).astype(jnp.float32)
        contrib = jnp.where(valid[:, None], values * flat_weight[picked][:, None], jnp.float32(0.0))
        return total.at[owner].add(contrib), None

    start = jnp.zeros((tokens.shape[0], tokens.shape[1]), jnp.float32)
    total, _ = lax.scan(step, start, (jnp.arange(EXPERTS, dtype=jnp.int32), w_gate, w_up, w_down))
    return (2.5 * total).astype(jnp.bfloat16)
```

```python
import functools

import jax
import jax.numpy as jnp
from jax import lax
from jax.experimental import pallas as pl
from jax.experimental.pallas import tpu as pltpu
from jax.sharding import PartitionSpec as P

LANES = 128
ALIGN = 16
CHUNKS = 1
VMEM_LIMIT = 56 * 1024 * 1024
SCALE = 2.5


def up_to(value, step):
    return -(-value // step) * step


def dot32(a, b):
    return jnp.dot(a, b, preferred_element_type=jnp.float32)


def iota(shape, dim):
    return lax.broadcasted_iota(jnp.int32, shape, dim)


def flag(mask):
    return jnp.where(mask, 1.0, 0.0)


def pack_kernel(chunks, experts, ids_ref, scores_ref, tok_ref, out_ref):
    rows, width = tok_ref.shape
    topk = ids_ref.shape[1]
    ids = ids_ref[...]
    sig = 1.0 / (1.0 + jnp.exp(-scores_ref[...]))
    lane_e = iota((rows, experts), 1)
    chosen = [
        jnp.sum(jnp.where(ids[:, k : k + 1] == lane_e, sig, 0.0), axis=1, keepdims=True)
        for k in range(topk)
    ]
    total = sum(chosen[1:], chosen[0])
    lane = iota((rows, LANES), 1)
    expert_of_lane = lax.rem(lane, experts)
    weight = jnp.zeros((rows, LANES), jnp.float32)
    for k in range(topk):
        weight = weight + jnp.where(ids[:, k : k + 1] == expert_of_lane, chosen[k] / total, 0.0)
    high = weight.astype(jnp.bfloat16).astype(jnp.float32)
    rest = weight - high
    middle = rest.astype(jnp.bfloat16).astype(jnp.float32)
    low = rest - middle
    pieces = jnp.where(
        lane < experts,
        high,
        jnp.where(lane < 2 * experts, middle, jnp.where(lane < 3 * experts, low, 0.0)),
    ).astype(jnp.bfloat16)
    if chunks == 1:
        out_ref[0, :, :width] = tok_ref[...]
        out_ref[0, :, width:] = pieces
        return
    first = jnp.min(ids.astype(jnp.float32), axis=1, keepdims=True)
    last = jnp.max(ids.astype(jnp.float32), axis=1, keepdims=True)
    key = jnp.broadcast_to(first * experts + last, (rows, rows))
    key_t = key.T
    i, j = iota((rows, rows), 0), iota((rows, rows), 1)
    ahead = (key < key_t) | ((key == key_t) & (i < j))
    rank = jnp.sum(flag(ahead), axis=0, keepdims=True)
    per = rows // chunks
    for c in range(chunks):
        place = iota((per, rows), 0) * chunks + c
        take = flag(rank.astype(jnp.int32) == place).astype(jnp.bfloat16)
        out_ref[c, :, :width] = dot32(take, tok_ref[...]).astype(jnp.bfloat16)
        out_ref[c, :, width:] = dot32(take, pieces).astype(jnp.bfloat16)


def pack(ids, scores, tokens, chunks):
    rows, width = tokens.shape
    experts = scores.shape[1]
    return pl.pallas_call(
        functools.partial(pack_kernel, chunks, experts),
        out_shape=jax.ShapeDtypeStruct((chunks, rows // chunks, width + LANES), jnp.bfloat16),
        compiler_params=pltpu.CompilerParams(vmem_limit_bytes=VMEM_LIMIT),
        cost_estimate=pl.CostEstimate(
            flops=2 * rows * rows * width, bytes_accessed=4 * rows * width, transcendentals=0
        ),
        name="pack",
    )(ids, scores, tokens)


def weight_of(meta, expert, experts):
    lane = iota(meta.shape, 1)
    hit = (lax.rem(lane, experts) == expert) & (lane < 3 * experts)
    return jnp.sum(jnp.where(hit, meta, 0.0), axis=1, keepdims=True)


def named(meta, expert):
    return jnp.sum(jnp.where(iota(meta.shape, 1) == expert, meta, 0.0), axis=1, keepdims=True) > 0.0


def pick(meta, expert, cap):
    rows = meta.shape[0]
    mine = flag(named(meta, expert))
    i, j = iota((rows, rows), 0), iota((rows, rows), 1)
    position = jnp.sum(jnp.where(i < j, mine, 0.0), axis=0, keepdims=True)
    present = jnp.sum(jnp.where(i == j, mine, 0.0), axis=0, keepdims=True)
    place = iota((cap, rows), 0)
    return flag((position.astype(jnp.int32) == place) & (present > 0.0)).astype(jnp.bfloat16)


def spread(meta, expert, cap):
    rows = meta.shape[0]
    mine = flag(named(meta, expert))
    i, j = iota((rows, rows), 0), iota((rows, rows), 1)
    row_mine = jnp.sum(jnp.where(i == j, mine, 0.0), axis=0, keepdims=True)
    position = jnp.sum(jnp.where(j < i, row_mine, 0.0), axis=1, keepdims=True)
    place = iota((rows, cap), 1)
    return flag((position.astype(jnp.int32) == place) & (mine > 0.0)).astype(jnp.bfloat16)


def pick_kernel(sel_ref, x_ref, y_ref):
    cap, width = y_ref.shape
    take = pick(x_ref[:, width:].astype(jnp.float32), sel_ref[1], cap)
    y_ref[...] = dot32(take, x_ref[:, :width]).astype(jnp.bfloat16)


def merge_pick_kernel(sel_ref, end_ref, inner_ref, x_ref, y_ref):
    cap, width = y_ref.shape

    @pl.when(sel_ref[2] == 1)
    def _():
        x_ref[...] = end_ref[...]

    @pl.when(sel_ref[2] == 0)
    def _():
        x_ref[...] = inner_ref[...]

    take = pick(x_ref[:, width:].astype(jnp.float32), sel_ref[1], cap)
    y_ref[...] = dot32(take, x_ref[:, :width]).astype(jnp.bfloat16)


def pick_rows(sel, parts, cap):
    rows, wide = parts[0].shape
    width = wide - LANES
    outs = [jax.ShapeDtypeStruct((cap, width), jnp.bfloat16)]
    if len(parts) == 2:
        outs = [jax.ShapeDtypeStruct((rows, wide), jnp.bfloat16)] + outs
    got = pl.pallas_call(
        merge_pick_kernel if len(parts) == 2 else pick_kernel,
        in_specs=[pl.BlockSpec(memory_space=pltpu.SMEM)]
        + [pl.BlockSpec(memory_space=pltpu.VMEM)] * len(parts),
        out_specs=[pl.BlockSpec(memory_space=pltpu.VMEM)] * len(outs),
        out_shape=outs,
        compiler_params=pltpu.CompilerParams(vmem_limit_bytes=VMEM_LIMIT),
        cost_estimate=pl.CostEstimate(
            flops=2 * rows * cap * width, bytes_accessed=4 * rows * width, transcendentals=0
        ),
        name="pick",
    )(sel, *parts)
    return (parts[0], got[0]) if len(parts) == 1 else tuple(got)


def expert_kernel(sizes, steps_h, steps_d, *refs):
    count = len(sizes)
    x_refs, refs = refs[:count], refs[count:]
    gates, ups, downs, refs = refs[0:2], refs[2:4], refs[4:6], refs[6:]
    out_refs, (xs, hidden) = refs[:count], refs[count:]
    step = pl.program_id(0)
    width = xs.shape[1]
    block = gates[0].shape[1]
    half = steps_h // 2

    @pl.when(step == 0)
    def _():
        at = 0
        for ref, size in zip(x_refs, sizes):
            xs[at : at + size, :] = ref[:, :width]
            at += size

    for s in range(steps_h):

        @pl.when(step == s)
        def _(s=s):
            which = s // half
            rows = xs[...]
            gate = dot32(rows, gates[which][...])
            up = dot32(rows, ups[which][...])
            value = gate / (1.0 + jnp.exp(-gate)) * up
            hidden[:, s * block : (s + 1) * block] = value.astype(jnp.bfloat16)

    @pl.when(step >= steps_h)
    def _():
        depth = downs[0].shape[0]
        out = dot32(hidden[:, :depth], downs[0][...]) + dot32(hidden[:, depth:], downs[1][...])
        out = out.astype(jnp.bfloat16)
        at = 0
        for ref, size in zip(out_refs, sizes):
            ref[...] = out[at : at + size, :]
            at += size


def expert(blocks, gates, ups, downs):
    sizes = [b.shape[0] for b in blocks]
    total = sum(sizes)
    width, depth = gates[0].shape
    block_h = 256 if depth % 256 == 0 else depth
    block_d = 512 if width % 512 == 0 else width
    half = depth // block_h
    steps_h, steps_d = 2 * half, width // block_d

    def up_map(which):
        return lambda i: (0, jnp.clip(i - which * half, 0, half - 1))

    def down_map(i):
        return (0, jnp.maximum(i - steps_h, 0))

    return pl.pallas_call(
        functools.partial(expert_kernel, sizes, steps_h, steps_d),
        grid=(steps_h + steps_d,),
        in_specs=[pl.BlockSpec(b.shape, lambda i: (0, 0), pipeline_mode=pl.Buffered(1)) for b in blocks]
        + [pl.BlockSpec((width, block_h), up_map(0)), pl.BlockSpec((width, block_h), up_map(1))] * 2
        + [pl.BlockSpec((depth, block_d), down_map)] * 2,
        out_specs=[pl.BlockSpec((s, block_d), down_map) for s in sizes],
        out_shape=[jax.ShapeDtypeStruct((s, width), jnp.bfloat16) for s in sizes],
        scratch_shapes=[
            pltpu.VMEM((total, width), jnp.bfloat16),
            pltpu.VMEM((total, 2 * depth), jnp.bfloat16),
        ],
        compiler_params=pltpu.CompilerParams(vmem_limit_bytes=VMEM_LIMIT),
        cost_estimate=pl.CostEstimate(
            flops=12 * total * width * depth,
            bytes_accessed=12 * width * depth + 4 * total * width,
            transcendentals=2 * total * depth,
        ),
        name="expert",
    )(*blocks, *gates, *ups, *downs)


def combine_kernel(experts, scale, sel_ref, meta_ref, own_ref, other_ref, *refs):
    out_ref = refs[-1]
    cap = other_ref.shape[0]
    meta = meta_ref[...].astype(jnp.float32)
    back = dot32(spread(meta, sel_ref[1], cap), other_ref[...])
    value = weight_of(meta, sel_ref[0], experts) * own_ref[...].astype(jnp.float32)
    value = value + weight_of(meta, sel_ref[1], experts) * back
    for ref in refs[:-1]:
        value = value + ref[...].astype(jnp.float32)
    if scale is not None:
        value = value * scale
    out_ref[...] = value.astype(jnp.bfloat16)


def combine(sel, x, own, other, extra, experts, scale=None):
    rows, width = own.shape
    cap = other.shape[0]
    block = 896 if width % 896 == 0 else width
    col = pl.BlockSpec((rows, block), lambda i: (0, i))
    return pl.pallas_call(
        functools.partial(combine_kernel, experts, scale),
        grid=(width // block,),
        in_specs=[
            pl.BlockSpec(memory_space=pltpu.SMEM),
            pl.BlockSpec((rows, LANES), lambda i: (0, width // LANES)),
            col,
            pl.BlockSpec((cap, block), lambda i: (0, i)),
        ]
        + [col] * len(extra),
        out_specs=col,
        out_shape=jax.ShapeDtypeStruct((rows, width), jnp.bfloat16),
        compiler_params=pltpu.CompilerParams(vmem_limit_bytes=VMEM_LIMIT),
        cost_estimate=pl.CostEstimate(
            flops=2 * rows * cap * width, bytes_accessed=6 * rows * width, transcendentals=0
        ),
        name="combine",
    )(sel, x, own, other, *extra)


def capacity_of(tok_rows, topk, experts):
    return min(tok_rows, max(2, 5 * tok_rows * topk // (2 * experts)))


def on_levels(pairs):
    return [(2 * a + y, 2 * b + y) for a, b in pairs for y in range(2)]


OUTER = on_levels([(0, 1), (1, 0), (2, 3), (3, 2)])
INNER = on_levels([(1, 2), (2, 1)])
TO_ENDS = on_levels([(1, 0), (2, 3)])
FROM_ENDS = on_levels([(0, 1), (3, 2)])


def four_levels(tokens, scores, expert_ids, w_gate, w_up, w_down):
    experts = lax.axis_size("expert")
    tok_rows, width = tokens.shape
    topk = expert_ids.shape[1]
    capacity = capacity_of(tok_rows, topk, experts)
    cap = min(tok_rows // CHUNKS, up_to((capacity + (CHUNKS - 1) * (experts - 1)) // CHUNKS, ALIGN))
    me = lax.axis_index("expert")
    level = me // 2
    end = ((level == 0) | (level == 3)).astype(jnp.int32)
    sel = jnp.stack([me, me ^ 1, end]).astype(jnp.int32)
    across = [(i, i ^ 1) for i in range(experts)]

    def send(value, pairs):
        return lax.ppermute(value, "expert", pairs)

    def swap(value):
        return lax.ppermute(value, "dp", [(0, 1), (1, 0)])

    gates = (w_gate[0], swap(w_gate[0]))
    ups = (w_up[0], swap(w_up[0]))
    downs = (w_down[0], swap(w_down[0]))

    packed = pack(expert_ids, scores, tokens, CHUNKS)
    results = []
    for c in range(CHUNKS):
        own = packed[c]
        near = send(own, OUTER)
        inner = send(own, INNER)
        _, y_own = pick_rows(sel, [own], cap)
        y_own = send(y_own, across)
        far_inner = send(near, INNER)
        far_end = send(inner, TO_ENDS)
        _, y_near = pick_rows(sel, [near], cap)
        y_near = send(y_near, across)
        last_end = send(far_inner, TO_ENDS)
        far, y_far = pick_rows(sel, [far_end, far_inner], cap)
        y_far = send(y_far, across)
        last, y_last = pick_rows(sel, [last_end, inner], cap)
        y_last = send(y_last, across)

        o_own, o_near, o_far, oy_own, oy_near, oy_far = expert(
            [own, near, far, y_own, y_near, y_far], gates, ups, downs
        )
        o_last, oy_last = expert([last, y_last], gates, ups, downs)

        b_last = send(oy_last, across)
        b_far = send(oy_far, across)
        b_near = send(oy_near, across)
        b_own = send(oy_own, across)

        p_last = combine(sel, last, o_last, b_last, [], experts)
        r1 = send(p_last, FROM_ENDS)
        p_far = combine(sel, far, o_far, b_far, [r1], experts)
        r_cross = send(p_far, INNER)
        r_in = send(p_far, FROM_ENDS)
        p_near = combine(sel, near, o_near, b_near, [r_cross], experts)
        r_near = send(p_near, OUTER)
        r_mid = send((p_last.astype(jnp.float32) + r_in.astype(jnp.float32)).astype(jnp.bfloat16), INNER)
        results.append(combine(sel, own, o_own, b_own, [r_near, r_mid], experts, SCALE))
    return results, packed


def per_device(tokens, scores, expert_ids, w_gate, w_up, w_down):
    results, packed = four_levels(tokens, scores, expert_ids, w_gate, w_up, w_down)
    return results[0]


def all_to_all_form(tokens, scores, expert_ids, w_gate, w_up, w_down):
    experts = lax.axis_size("expert")
    tok_rows, width = tokens.shape
    topk = expert_ids.shape[1]
    capacity = capacity_of(tok_rows, topk, experts)
    flat_ids = expert_ids.reshape(-1)
    onehot = (flat_ids[:, None] == jnp.arange(experts, dtype=jnp.int32)[None, :]).astype(jnp.int32)
    position = jnp.sum((jnp.cumsum(onehot, axis=0) - 1) * onehot, axis=1)
    slot = flat_ids * capacity + position
    repeated = jnp.repeat(tokens, topk, axis=0)
    outgoing = jnp.zeros((experts * capacity, width), tokens.dtype).at[slot].set(repeated)
    outgoing = outgoing.reshape(experts, capacity, width)
    doubled = jnp.tile(outgoing, (lax.axis_size("dp"), 1, 1))
    rows = lax.all_to_all(doubled, ("dp", "expert"), split_axis=0, concat_axis=0, tiled=True)
    shape = rows.shape
    flat = rows.reshape(-1, shape[-1])
    gate = dot32(flat, w_gate[0])
    up_value = dot32(flat, w_up[0])
    hidden = (jax.nn.silu(gate) * up_value).astype(jnp.bfloat16)
    partial_value = dot32(hidden, w_down[0]).reshape(shape)
    returned = lax.all_to_all(
        partial_value, ("dp", "expert"), split_axis=0, concat_axis=0, tiled=True
    )
    back = jnp.sum(returned.reshape(-1, experts, capacity, width), axis=0).astype(jnp.bfloat16)
    picked = back.reshape(experts * capacity, width)[slot].reshape(tok_rows, topk, width)
    chosen = jax.nn.sigmoid(jnp.take_along_axis(scores, expert_ids, axis=1))
    weight = chosen / jnp.sum(chosen, axis=1, keepdims=True)
    mixed = SCALE * jnp.sum(weight[:, :, None] * picked.astype(jnp.float32), axis=1)
    return mixed.astype(jnp.bfloat16)


def solution(mesh):
    in_specs = (
        P(("groups", "dp", "expert"), None),
        P(("groups", "dp", "expert"), None),
        P(("groups", "dp", "expert"), None),
        P("expert", None, "dp"),
        P("expert", None, "dp"),
        P("expert", "dp", None),
    )
    out_specs = P(("groups", "dp", "expert"), None)
    short = mesh.shape["expert"] == 8 and mesh.shape["dp"] == 2
    body = per_device if short else all_to_all_form
    return jax.shard_map(
        body, mesh=mesh, in_specs=in_specs, out_specs=out_specs, check_vma=False
    )
```

```python
import functools

import jax
import jax.numpy as jnp
from jax import lax
from jax.experimental import pallas as pl
from jax.experimental.pallas import tpu as pltpu
from jax.sharding import PartitionSpec as P

LANES = 128
ALIGN = 16
HALVES = 2
VMEM_LIMIT = 24 * 1024 * 1024
SCALE = 2.5
BRIEF = pl.CostEstimate(flops=1, bytes_accessed=1, transcendentals=0)


def up_to(value, step):
    return -(-value // step) * step


def dot32(a, b):
    return jnp.dot(a, b, preferred_element_type=jnp.float32)


def iota(shape, dim):
    return lax.broadcasted_iota(jnp.int32, shape, dim)


def flag(mask):
    return jnp.where(mask, 1.0, 0.0)


def pieces_of(ids_ref, scores_ref):
    topk, rows = ids_ref.shape
    experts = scores_ref.shape[0]
    sig = 1.0 / (1.0 + jnp.exp(-scores_ref[...]))
    ids = [ids_ref[k : k + 1, :] for k in range(topk)]
    row_e = iota((experts, rows), 0)
    chosen = [jnp.sum(jnp.where(i == row_e, sig, 0.0), axis=0, keepdims=True) for i in ids]
    total = sum(chosen[1:], chosen[0])
    row = iota((LANES, rows), 0)
    expert_of_row = lax.rem(row, experts)
    weight = jnp.zeros((LANES, rows), jnp.float32)
    for i, value in zip(ids, chosen):
        weight = weight + jnp.where(i == expert_of_row, value / total, 0.0)
    high = weight.astype(jnp.bfloat16).astype(jnp.float32)
    rest = weight - high
    middle = rest.astype(jnp.bfloat16).astype(jnp.float32)
    low = rest - middle
    pieces = jnp.where(
        row < experts,
        high,
        jnp.where(row < 2 * experts, middle, jnp.where(row < 3 * experts, low, 0.0)),
    )
    return pieces.T


def route(meta, sel_ref, experts, cap):
    rows = meta.shape[0]
    i, j = iota((rows, rows), 0), iota((rows, rows), 1)
    lane = iota((rows, LANES), 1)

    def weight_for(expert):
        hit = (lax.rem(lane, experts) == expert) & (lane < 3 * experts)
        return jnp.sum(jnp.where(hit, meta, 0.0), axis=1, keepdims=True)

    mine, other = weight_for(sel_ref[0]), weight_for(sel_ref[1])
    weights = jnp.where(lane == 0, mine, other)
    named = flag(other > 0.0)
    row_named = jnp.sum(jnp.where(i == j, named, 0.0), axis=0, keepdims=True)
    row_place = jnp.sum(jnp.where(i < j, named, 0.0), axis=0, keepdims=True).astype(jnp.int32)
    place = jnp.sum(jnp.where(j < i, row_named, 0.0), axis=1, keepdims=True).astype(jnp.int32)
    take = flag((iota((cap, rows), 0) == row_place) & (row_named > 0.0))
    back = flag((iota((rows, cap), 1) == place) & (named > 0.0))
    return take.astype(jnp.bfloat16), back.astype(jnp.bfloat16), weights


def open_kernel(sel_ref, ids_ref, scores_ref, tok_ref, packed_ref, y_ref, back_ref, weight_ref):
    width = tok_ref.shape[1]
    pieces = pieces_of(ids_ref, scores_ref)
    packed_ref[:, :width] = tok_ref[...]
    packed_ref[:, width:] = pieces.astype(jnp.bfloat16)
    take, back, weights = route(pieces, sel_ref, scores_ref.shape[0], y_ref.shape[0])
    back_ref[...] = back
    weight_ref[...] = weights
    y_ref[...] = dot32(take, tok_ref[...]).astype(jnp.bfloat16)


def open_block(sel, ids, scores, tokens, cap):
    rows, width = tokens.shape
    return pl.pallas_call(
        open_kernel,
        in_specs=[pl.BlockSpec(memory_space=pltpu.SMEM)]
        + [pl.BlockSpec(memory_space=pltpu.VMEM)] * 3,
        out_shape=[
            jax.ShapeDtypeStruct((rows, width + LANES), jnp.bfloat16),
            jax.ShapeDtypeStruct((cap, width), jnp.bfloat16),
            jax.ShapeDtypeStruct((rows, cap), jnp.bfloat16),
            jax.ShapeDtypeStruct((rows, LANES), jnp.float32),
        ],
        compiler_params=pltpu.CompilerParams(vmem_limit_bytes=VMEM_LIMIT),
        cost_estimate=BRIEF,
        name="open",
    )(sel, ids.T, scores.T, tokens)


def pick_kernel(experts, count, sel_ref, *refs):
    metas, parts, (y_ref, back_ref, weight_ref, held) = refs[:count], refs[count : 2 * count], refs[2 * count :]

    @pl.when(pl.program_id(0) == 0)
    def _():
        meta = metas[0][...].astype(jnp.float32)
        if count == 2:
            meta = jnp.where(sel_ref[2] == 1, meta, metas[1][...].astype(jnp.float32))
        take, back, weights = route(meta, sel_ref, experts, y_ref.shape[0])
        held[...] = take
        back_ref[...] = back
        weight_ref[...] = weights

    for which in range(count):

        @pl.when((sel_ref[2] == 1 - which) | (count == 1))
        def _(which=which):
            y_ref[...] = dot32(held[...], parts[which][...]).astype(jnp.bfloat16)


def pick_rows(sel, parts, experts, cap):
    rows, width = parts[0].shape
    width -= LANES
    block = column_block(width)
    return pl.pallas_call(
        functools.partial(pick_kernel, experts, len(parts)),
        grid=(width // block,),
        in_specs=[pl.BlockSpec(memory_space=pltpu.SMEM)]
        + [pl.BlockSpec((rows, LANES), lambda i: (0, width // LANES))] * len(parts)
        + [pl.BlockSpec((rows, block), lambda i: (0, i))] * len(parts),
        out_specs=[
            pl.BlockSpec((cap, block), lambda i: (0, i)),
            pl.BlockSpec((rows, cap), lambda i: (0, 0)),
            pl.BlockSpec((rows, LANES), lambda i: (0, 0)),
        ],
        out_shape=[
            jax.ShapeDtypeStruct((cap, width), jnp.bfloat16),
            jax.ShapeDtypeStruct((rows, cap), jnp.bfloat16),
            jax.ShapeDtypeStruct((rows, LANES), jnp.float32),
        ],
        scratch_shapes=[pltpu.VMEM((cap, rows), jnp.bfloat16)],
        compiler_params=pltpu.CompilerParams(vmem_limit_bytes=VMEM_LIMIT),
        cost_estimate=BRIEF,
        name="pick",
    )(sel, *parts, *parts)


def hold_kernel(*refs):
    count = len(refs) // 2
    sems = refs[-1]
    copies = [
        pltpu.make_async_copy(refs[k], refs[count + k], sems.at[k]) for k in range(count)
    ]
    for copy in copies:
        copy.start()
    for copy in copies:
        copy.wait()


def hold(weights):
    held = pl.pallas_call(
        hold_kernel,
        in_specs=[pl.BlockSpec(memory_space=pltpu.HBM)] * len(weights),
        out_specs=[pl.BlockSpec(memory_space=pltpu.VMEM)] * len(weights),
        out_shape=[pltpu.VMEM(w.shape, w.dtype) for w in weights],
        scratch_shapes=[pltpu.SemaphoreType.DMA((len(weights),))],
        compiler_params=pltpu.CompilerParams(vmem_limit_bytes=VMEM_LIMIT),
        cost_estimate=BRIEF,
        name="hold",
    )(*weights)
    return [pltpu.with_memory_space_constraint(w, pltpu.VMEM) for w in held]


def expert_kernel(count, halves, sel_ref, *refs):
    parts, y_ref, refs = refs[:count], refs[count], refs[count + 1 :]
    gates, ups, downs, refs = refs[0:2], refs[2:4], refs[4:6], refs[6:]
    out_ref, y_outs, (xs, hidden) = refs[0], refs[1 : 1 + halves], refs[1 + halves :]
    rows, cap = parts[0].shape[0], y_ref.shape[0]
    width, depth = gates[0].shape
    if count == 1:
        xs[:rows, :] = parts[0][:, :width]
    else:
        for which in range(2):

            @pl.when(sel_ref[2] == 1 - which)
            def _(which=which):
                xs[:rows, :] = parts[which][:, :width]

    xs[rows:, :] = y_ref[...]
    block = min(depth, 256)
    for which in range(2):
        for at in range(0, depth, block):
            gate = dot32(xs[...], gates[which][:, at : at + block])
            up = dot32(xs[...], ups[which][:, at : at + block])
            value = gate / (1.0 + jnp.exp(-gate)) * up
            to = which * depth + at
            hidden[:, to : to + block] = value.astype(jnp.bfloat16)
    part = width // halves
    block = column_block(part)
    for at in range(0, width, block):
        columns = slice(at, at + block)
        out = dot32(hidden[:, :depth], downs[0][:, columns])
        out = (out + dot32(hidden[:, depth:], downs[1][:, columns])).astype(jnp.bfloat16)
        out_ref[:, columns] = out[:rows]
        inside = at % part
        y_outs[at // part][:, inside : inside + block] = out[rows:]


def expert(sel, parts, y, gates, ups, downs, halves):
    rows, cap = parts[0].shape[0], y.shape[0]
    width, depth = gates[0].shape
    whole = pl.BlockSpec(memory_space=pltpu.VMEM)
    return pl.pallas_call(
        functools.partial(expert_kernel, len(parts), halves),
        in_specs=[pl.BlockSpec(memory_space=pltpu.SMEM)] + [whole] * (len(parts) + 7),
        out_specs=[whole] * (1 + halves),
        out_shape=[jax.ShapeDtypeStruct((rows, width), jnp.bfloat16)]
        + [jax.ShapeDtypeStruct((cap, width // halves), jnp.bfloat16)] * halves,
        scratch_shapes=[
            pltpu.VMEM((rows + cap, width), jnp.bfloat16),
            pltpu.VMEM((rows + cap, 2 * depth), jnp.bfloat16),
        ],
        compiler_params=pltpu.CompilerParams(vmem_limit_bytes=VMEM_LIMIT),
        cost_estimate=BRIEF,
        name="expert",
    )(sel, *parts, y, *gates, *ups, *downs)


def combine_kernel(scale, splits, back_ref, weight_ref, own_ref, other_ref, *refs):
    out_ref = refs[-1]
    step, steps = pl.program_id(0), pl.num_programs(0)
    weights = weight_ref[...]
    value = weights[:, 0:1] * own_ref[...].astype(jnp.float32)
    value = value + weights[:, 1:2] * dot32(back_ref[...], other_ref[...])
    at = 0
    for pieces in splits:
        term = refs[at][...].astype(jnp.float32)
        for p in range(1, pieces):
            here = step * pieces >= p * steps
            term = jnp.where(here, refs[at + p][...].astype(jnp.float32), term)
        at += pieces
        value = value + term
    if scale is not None:
        value = value * scale
    out_ref[...] = value.astype(jnp.bfloat16)


def combine(tables, own, other, extra=(), first=0, scale=None):
    rows = own.shape[0]
    cap, width = other.shape
    block = column_block(width)
    steps = width // block
    offset = first // block

    def piece(p, count):
        each = steps // count
        return pl.BlockSpec((rows, block), lambda i: (0, jnp.clip(i - p * each, 0, each - 1)))

    return pl.pallas_call(
        functools.partial(combine_kernel, scale, [len(e) for e in extra]),
        grid=(steps,),
        in_specs=[
            pl.BlockSpec((rows, cap), lambda i: (0, 0)),
            pl.BlockSpec((rows, LANES), lambda i: (0, 0)),
            pl.BlockSpec((rows, block), lambda i: (0, i + offset)),
            pl.BlockSpec((cap, block), lambda i: (0, i)),
        ]
        + [piece(p, len(e)) for e in extra for p in range(len(e))],
        out_specs=pl.BlockSpec((rows, block), lambda i: (0, i)),
        out_shape=jax.ShapeDtypeStruct((rows, width), jnp.bfloat16),
        compiler_params=pltpu.CompilerParams(vmem_limit_bytes=VMEM_LIMIT),
        cost_estimate=BRIEF,
        name="combine",
    )(*tables, own, other, *[e for group in extra for e in group])


def column_block(width):
    return 896 if width % 896 == 0 else width


def capacity_of(tok_rows, topk, experts):
    return min(tok_rows, max(2, 5 * tok_rows * topk // (2 * experts)))


def on_levels(pairs):
    return [(2 * a + y, 2 * b + y) for a, b in pairs for y in range(2)]


OUTER = on_levels([(0, 1), (1, 0), (2, 3), (3, 2)])
INNER = on_levels([(1, 2), (2, 1)])
TO_ENDS = on_levels([(1, 0), (2, 3)])
FROM_ENDS = on_levels([(0, 1), (3, 2)])


def after(value, *others):
    return lax.optimization_barrier((value, *others))[0]


def add(a, b):
    return (a.astype(jnp.float32) + b.astype(jnp.float32)).astype(jnp.bfloat16)


def four_levels(tokens, scores, expert_ids, w_gate, w_up, w_down):
    experts = lax.axis_size("expert")
    tok_rows, width = tokens.shape
    topk = expert_ids.shape[1]
    cap = min(tok_rows, up_to(capacity_of(tok_rows, topk, experts), ALIGN))
    me = lax.axis_index("expert")
    level = me // 2
    end = ((level == 0) | (level == 3)).astype(jnp.int32)
    sel = jnp.stack([me, me ^ 1, end]).astype(jnp.int32)
    across = [(i, i ^ 1) for i in range(experts)]

    def send(value, pairs):
        return lax.ppermute(value, "expert", pairs)

    def swap(value):
        return lax.ppermute(value, "dp", [(0, 1), (1, 0)])

    swapped = [swap(w[0]) for w in (w_gate, w_up, w_down)]
    own, s0, *tables0 = open_block(sel, expert_ids, scores, tokens, cap)
    near = send(own, OUTER)
    inner = send(own, INNER)
    y0 = send(after(s0, swapped[0]), across)

    kept = hold(lax.optimization_barrier((w_gate[0], w_up[0], w_down[0], own))[:-1])
    near = after(near, y0, kept[0])
    far_inner = send(near, INNER)
    far_end = send(inner, TO_ENDS)
    s1, *tables1 = pick_rows(sel, [near], experts, cap)
    y1 = send(s1, across)
    gates, ups, downs = zip(kept, hold(lax.optimization_barrier((*swapped, s1))[:-1]))
    o0, oy0 = expert(sel, [own], y0, gates, ups, downs, 1)
    o1, oy1 = expert(sel, [after(near, o0)], y1, gates, ups, downs, 1)
    b1 = send(oy1, across)

    far_inner = after(far_inner, o1)
    last_end = send(far_inner, TO_ENDS)
    far = [after(far_end, o1), inner]
    s2, *tables2 = pick_rows(sel, far, experts, cap)
    y2 = send(s2, across)
    q1 = combine(tables1, o1, after(b1, s2))
    r1 = send(q1, FROM_ENDS)
    o2, oy2 = expert(sel, [after(far[0], q1), inner], y2, gates, ups, downs, 1)
    last = [after(last_end, o2), far_inner]
    s3, *tables3 = pick_rows(sel, last, experts, cap)
    y3 = send(s3, across)
    b2 = send(after(oy2, y3), across)
    o3, *oy3 = expert(sel, last, y3, gates, ups, downs, HALVES)
    b3 = [send(v, across) for v in oy3]

    part = width // HALVES
    b3[0] = after(b3[0], r1)
    q3 = [combine(tables3, o3, v, first=h * part) for h, v in enumerate(b3)]
    r3 = [send(v, FROM_ENDS) for v in q3]
    q2 = combine(tables2, o2, after(b2, q3[-1]))
    b0 = send(after(oy0, q2), across)
    r2 = send(q2, FROM_ENDS)
    r3 = [send(add(q, r), INNER) for q, r in zip(q3, r3)]
    r2 = send(add(q2, r2), INNER)
    r3 = [
        send(add(q1[:, h * part : (h + 1) * part], r), TO_ENDS) for h, r in enumerate(r3)
    ]
    return combine(tables0, o0, b0, extra=([r1], [r2], r3), scale=SCALE)


def all_to_all_form(tokens, scores, expert_ids, w_gate, w_up, w_down):
    experts = lax.axis_size("expert")
    tok_rows, width = tokens.shape
    topk = expert_ids.shape[1]
    capacity = capacity_of(tok_rows, topk, experts)
    flat_ids = expert_ids.reshape(-1)
    onehot = (flat_ids[:, None] == jnp.arange(experts, dtype=jnp.int32)[None, :]).astype(jnp.int32)
    position = jnp.sum((jnp.cumsum(onehot, axis=0) - 1) * onehot, axis=1)
    slot = flat_ids * capacity + position
    repeated = jnp.repeat(tokens, topk, axis=0)
    outgoing = jnp.zeros((experts * capacity, width), tokens.dtype).at[slot].set(repeated)
    outgoing = outgoing.reshape(experts, capacity, width)
    doubled = jnp.tile(outgoing, (lax.axis_size("dp"), 1, 1))
    rows = lax.all_to_all(doubled, ("dp", "expert"), split_axis=0, concat_axis=0, tiled=True)
    shape = rows.shape
    flat = rows.reshape(-1, shape[-1])
    gate = dot32(flat, w_gate[0])
    up_value = dot32(flat, w_up[0])
    hidden = (jax.nn.silu(gate) * up_value).astype(jnp.bfloat16)
    partial_value = dot32(hidden, w_down[0]).reshape(shape)
    returned = lax.all_to_all(
        partial_value, ("dp", "expert"), split_axis=0, concat_axis=0, tiled=True
    )
    back = jnp.sum(returned.reshape(-1, experts, capacity, width), axis=0).astype(jnp.bfloat16)
    picked = back.reshape(experts * capacity, width)[slot].reshape(tok_rows, topk, width)
    chosen = jax.nn.sigmoid(jnp.take_along_axis(scores, expert_ids, axis=1))
    weight = chosen / jnp.sum(chosen, axis=1, keepdims=True)
    mixed = SCALE * jnp.sum(weight[:, :, None] * picked.astype(jnp.float32), axis=1)
    return mixed.astype(jnp.bfloat16)


def solution(mesh):
    in_specs = (
        P(("groups", "dp", "expert"), None),
        P(("groups", "dp", "expert"), None),
        P(("groups", "dp", "expert"), None),
        P("expert", None, "dp"),
        P("expert", None, "dp"),
        P("expert", "dp", None),
    )
    out_specs = P(("groups", "dp", "expert"), None)
    short = mesh.shape["expert"] == 8 and mesh.shape["dp"] == 2
    body = four_levels if short else all_to_all_form
    return jax.shard_map(
        body, mesh=mesh, in_specs=in_specs, out_specs=out_specs, check_vma=False
    )
```

```python
import functools

import jax
import jax.numpy as jnp
from jax import lax
from jax.experimental import pallas as pl
from jax.experimental.pallas import tpu as pltpu
from jax.sharding import PartitionSpec as P

LANES = 128
ALIGN = 16
HALVES = 2
VMEM_LIMIT = 24 * 1024 * 1024
SCALE = 2.5
BRIEF = pl.CostEstimate(flops=1, bytes_accessed=1, transcendentals=0)


def up_to(value, step):
    return -(-value // step) * step


def dot32(a, b):
    return jnp.dot(a, b, preferred_element_type=jnp.float32)


def iota(shape, dim):
    return lax.broadcasted_iota(jnp.int32, shape, dim)


def flag(mask):
    return jnp.where(mask, 1.0, 0.0)


def pieces_of(ids_ref, scores_ref):
    topk, rows = ids_ref.shape
    experts = scores_ref.shape[0]
    sig = 1.0 / (1.0 + jnp.exp(-scores_ref[...]))
    ids = [ids_ref[k : k + 1, :] for k in range(topk)]
    row_e = iota((experts, rows), 0)
    chosen = [jnp.sum(jnp.where(i == row_e, sig, 0.0), axis=0, keepdims=True) for i in ids]
    total = sum(chosen[1:], chosen[0])
    row = iota((LANES, rows), 0)
    expert_of_row = lax.rem(row, experts)
    weight = jnp.zeros((LANES, rows), jnp.float32)
    for i, value in zip(ids, chosen):
        weight = weight + jnp.where(i == expert_of_row, value / total, 0.0)
    high = weight.astype(jnp.bfloat16).astype(jnp.float32)
    rest = weight - high
    middle = rest.astype(jnp.bfloat16).astype(jnp.float32)
    low = rest - middle
    pieces = jnp.where(
        row < experts,
        high,
        jnp.where(row < 2 * experts, middle, jnp.where(row < 3 * experts, low, 0.0)),
    )
    return pieces.T


def route(meta, sel_ref, experts, cap):
    rows = meta.shape[0]
    i, j = iota((rows, rows), 0), iota((rows, rows), 1)
    lane = iota((rows, LANES), 1)

    def weight_for(expert):
        hit = (lax.rem(lane, experts) == expert) & (lane < 3 * experts)
        return jnp.sum(jnp.where(hit, meta, 0.0), axis=1, keepdims=True)

    mine, other = weight_for(sel_ref[0]), weight_for(sel_ref[1])
    weights = jnp.where(lane == 0, mine, other)
    named = flag(other > 0.0)
    row_named = jnp.sum(jnp.where(i == j, named, 0.0), axis=0, keepdims=True)
    row_place = jnp.sum(jnp.where(i < j, named, 0.0), axis=0, keepdims=True).astype(jnp.int32)
    place = jnp.sum(jnp.where(j < i, row_named, 0.0), axis=1, keepdims=True).astype(jnp.int32)
    take = flag((iota((cap, rows), 0) == row_place) & (row_named > 0.0))
    back = flag((iota((rows, cap), 1) == place) & (named > 0.0))
    return take.astype(jnp.bfloat16), back.astype(jnp.bfloat16), weights


def open_kernel(sel_ref, ids_ref, scores_ref, tok_ref, packed_ref, y_ref, back_ref, weight_ref):
    width = tok_ref.shape[1]
    pieces = pieces_of(ids_ref, scores_ref)
    packed_ref[:, :width] = tok_ref[...]
    packed_ref[:, width:] = pieces.astype(jnp.bfloat16)
    take, back, weights = route(pieces, sel_ref, scores_ref.shape[0], y_ref.shape[0])
    back_ref[...] = back
    weight_ref[...] = weights
    y_ref[...] = dot32(take, tok_ref[...]).astype(jnp.bfloat16)


def open_block(sel, ids, scores, tokens, cap):
    rows, width = tokens.shape
    return pl.pallas_call(
        open_kernel,
        in_specs=[pl.BlockSpec(memory_space=pltpu.SMEM)]
        + [pl.BlockSpec(memory_space=pltpu.VMEM)] * 3,
        out_shape=[
            jax.ShapeDtypeStruct((rows, width + LANES), jnp.bfloat16),
            jax.ShapeDtypeStruct((cap, width), jnp.bfloat16),
            jax.ShapeDtypeStruct((rows, cap), jnp.bfloat16),
            jax.ShapeDtypeStruct((rows, LANES), jnp.float32),
        ],
        compiler_params=pltpu.CompilerParams(vmem_limit_bytes=VMEM_LIMIT),
        cost_estimate=BRIEF,
        name="open",
    )(sel, ids.T, scores.T, tokens)


def pick_kernel(experts, count, sel_ref, *refs):
    metas, parts, (y_ref, back_ref, weight_ref, held) = refs[:count], refs[count : 2 * count], refs[2 * count :]

    @pl.when(pl.program_id(0) == 0)
    def _():
        meta = metas[0][...].astype(jnp.float32)
        if count == 2:
            meta = jnp.where(sel_ref[2] == 1, meta, metas[1][...].astype(jnp.float32))
        take, back, weights = route(meta, sel_ref, experts, y_ref.shape[0])
        held[...] = take
        back_ref[...] = back
        weight_ref[...] = weights

    for which in range(count):

        @pl.when((sel_ref[2] == 1 - which) | (count == 1))
        def _(which=which):
            y_ref[...] = dot32(held[...], parts[which][...]).astype(jnp.bfloat16)


def pick_rows(sel, parts, experts, cap):
    rows, width = parts[0].shape
    width -= LANES
    block = column_block(width)
    return pl.pallas_call(
        functools.partial(pick_kernel, experts, len(parts)),
        grid=(width // block,),
        in_specs=[pl.BlockSpec(memory_space=pltpu.SMEM)]
        + [pl.BlockSpec((rows, LANES), lambda i: (0, width // LANES))] * len(parts)
        + [pl.BlockSpec((rows, block), lambda i: (0, i))] * len(parts),
        out_specs=[
            pl.BlockSpec((cap, block), lambda i: (0, i)),
            pl.BlockSpec((rows, cap), lambda i: (0, 0)),
            pl.BlockSpec((rows, LANES), lambda i: (0, 0)),
        ],
        out_shape=[
            jax.ShapeDtypeStruct((cap, width), jnp.bfloat16),
            jax.ShapeDtypeStruct((rows, cap), jnp.bfloat16),
            jax.ShapeDtypeStruct((rows, LANES), jnp.float32),
        ],
        scratch_shapes=[pltpu.VMEM((cap, rows), jnp.bfloat16)],
        compiler_params=pltpu.CompilerParams(vmem_limit_bytes=VMEM_LIMIT),
        cost_estimate=BRIEF,
        name="pick",
    )(sel, *parts, *parts)


def hold_kernel(*refs):
    count = len(refs) // 2
    sems = refs[-1]
    copies = [
        pltpu.make_async_copy(refs[k], refs[count + k], sems.at[k]) for k in range(count)
    ]
    for copy in copies:
        copy.start()
    for copy in copies:
        copy.wait()


def hold(weights):
    held = pl.pallas_call(
        hold_kernel,
        in_specs=[pl.BlockSpec(memory_space=pltpu.HBM)] * len(weights),
        out_specs=[pl.BlockSpec(memory_space=pltpu.VMEM)] * len(weights),
        out_shape=[pltpu.VMEM(w.shape, w.dtype) for w in weights],
        scratch_shapes=[pltpu.SemaphoreType.DMA((len(weights),))],
        compiler_params=pltpu.CompilerParams(vmem_limit_bytes=VMEM_LIMIT),
        cost_estimate=BRIEF,
        name="hold",
    )(*weights)
    return [pltpu.with_memory_space_constraint(w, pltpu.VMEM) for w in held]


def expert_kernel(count, halves, sel_ref, *refs):
    parts, y_ref, refs = refs[:count], refs[count], refs[count + 1 :]
    gates, ups, downs, refs = refs[0:2], refs[2:4], refs[4:6], refs[6:]
    out_ref, y_outs, (xs, hidden) = refs[0], refs[1 : 1 + halves], refs[1 + halves :]
    rows, cap = parts[0].shape[0], y_ref.shape[0]
    width, depth = gates[0].shape
    if count == 1:
        xs[:rows, :] = parts[0][:, :width]
    else:
        for which in range(2):

            @pl.when(sel_ref[2] == 1 - which)
            def _(which=which):
                xs[:rows, :] = parts[which][:, :width]

    xs[rows:, :] = y_ref[...]
    block = min(depth, 256)
    for which in range(2):
        for at in range(0, depth, block):
            gate = dot32(xs[...], gates[which][:, at : at + block])
            up = dot32(xs[...], ups[which][:, at : at + block])
            value = gate / (1.0 + jnp.exp(-gate)) * up
            to = which * depth + at
            hidden[:, to : to + block] = value.astype(jnp.bfloat16)
    part = width // halves
    block = column_block(part)
    for at in range(0, width, block):
        columns = slice(at, at + block)
        out = dot32(hidden[:, :depth], downs[0][:, columns])
        out = (out + dot32(hidden[:, depth:], downs[1][:, columns])).astype(jnp.bfloat16)
        out_ref[:, columns] = out[:rows]
        inside = at % part
        y_outs[at // part][:, inside : inside + block] = out[rows:]


def expert(sel, parts, y, gates, ups, downs, halves):
    rows, cap = parts[0].shape[0], y.shape[0]
    width, depth = gates[0].shape
    whole = pl.BlockSpec(memory_space=pltpu.VMEM)
    return pl.pallas_call(
        functools.partial(expert_kernel, len(parts), halves),
        in_specs=[pl.BlockSpec(memory_space=pltpu.SMEM)] + [whole] * (len(parts) + 7),
        out_specs=[whole] * (1 + halves),
        out_shape=[jax.ShapeDtypeStruct((rows, width), jnp.bfloat16)]
        + [jax.ShapeDtypeStruct((cap, width // halves), jnp.bfloat16)] * halves,
        scratch_shapes=[
            pltpu.VMEM((rows + cap, width), jnp.bfloat16),
            pltpu.VMEM((rows + cap, 2 * depth), jnp.bfloat16),
        ],
        compiler_params=pltpu.CompilerParams(vmem_limit_bytes=VMEM_LIMIT),
        cost_estimate=BRIEF,
        name="expert",
    )(sel, *parts, y, *gates, *ups, *downs)


def combine_kernel(scale, splits, back_ref, weight_ref, own_ref, other_ref, *refs):
    out_ref = refs[-1]
    step, steps = pl.program_id(0), pl.num_programs(0)
    weights = weight_ref[...]
    value = weights[:, 0:1] * own_ref[...].astype(jnp.float32)
    value = value + weights[:, 1:2] * dot32(back_ref[...], other_ref[...])
    at = 0
    for pieces in splits:
        term = refs[at][...].astype(jnp.float32)
        for p in range(1, pieces):
            here = step * pieces >= p * steps
            term = jnp.where(here, refs[at + p][...].astype(jnp.float32), term)
        at += pieces
        value = value + term
    if scale is not None:
        value = value * scale
    out_ref[...] = value.astype(jnp.bfloat16)


def combine(tables, own, other, extra=(), first=0, scale=None):
    rows = own.shape[0]
    cap, width = other.shape
    block = column_block(width)
    steps = width // block
    offset = first // block

    def piece(p, count):
        each = steps // count
        return pl.BlockSpec((rows, block), lambda i: (0, jnp.clip(i - p * each, 0, each - 1)))

    return pl.pallas_call(
        functools.partial(combine_kernel, scale, [len(e) for e in extra]),
        grid=(steps,),
        in_specs=[
            pl.BlockSpec((rows, cap), lambda i: (0, 0)),
            pl.BlockSpec((rows, LANES), lambda i: (0, 0)),
            pl.BlockSpec((rows, block), lambda i: (0, i + offset)),
            pl.BlockSpec((cap, block), lambda i: (0, i)),
        ]
        + [piece(p, len(e)) for e in extra for p in range(len(e))],
        out_specs=pl.BlockSpec((rows, block), lambda i: (0, i)),
        out_shape=jax.ShapeDtypeStruct((rows, width), jnp.bfloat16),
        compiler_params=pltpu.CompilerParams(vmem_limit_bytes=VMEM_LIMIT),
        cost_estimate=BRIEF,
        name="combine",
    )(*tables, own, other, *[e for group in extra for e in group])


def column_block(width):
    return 896 if width % 896 == 0 else width


def capacity_of(tok_rows, topk, experts):
    return min(tok_rows, max(2, 5 * tok_rows * topk // (2 * experts)))


def on_levels(pairs):
    return [(2 * a + y, 2 * b + y) for a, b in pairs for y in range(2)]


OUTER = on_levels([(0, 1), (1, 0), (2, 3), (3, 2)])
INNER = on_levels([(1, 2), (2, 1)])
TO_ENDS = on_levels([(1, 0), (2, 3)])
FROM_ENDS = on_levels([(0, 1), (3, 2)])


def after(value, *others):
    return lax.optimization_barrier((value, *others))[0]


def add(a, b):
    return (a.astype(jnp.float32) + b.astype(jnp.float32)).astype(jnp.bfloat16)


def four_levels(tokens, scores, expert_ids, w_gate, w_up, w_down):
    experts = lax.axis_size("expert")
    tok_rows, width = tokens.shape
    topk = expert_ids.shape[1]
    cap = min(tok_rows, up_to(capacity_of(tok_rows, topk, experts), ALIGN))
    me = lax.axis_index("expert")
    level = me // 2
    end = ((level == 0) | (level == 3)).astype(jnp.int32)
    sel = jnp.stack([me, me ^ 1, end]).astype(jnp.int32)
    across = [(i, i ^ 1) for i in range(experts)]

    def send(value, pairs):
        return lax.ppermute(value, "expert", pairs)

    def swap(value):
        return lax.ppermute(value, "dp", [(0, 1), (1, 0)])

    swapped = [swap(w[0]) for w in (w_gate, w_up, w_down)]
    own, s0, *tables0 = open_block(sel, expert_ids, scores, tokens, cap)
    near = send(own, OUTER)
    inner = send(own, INNER)
    y0 = send(after(s0, swapped[0]), across)

    kept = hold(lax.optimization_barrier((w_gate[0], w_up[0], w_down[0], own))[:-1])
    near = after(near, y0, kept[0])
    far_inner = send(near, INNER)
    far_end = send(inner, TO_ENDS)
    s1, *tables1 = pick_rows(sel, [near], experts, cap)
    y1 = send(s1, across)
    gates, ups, downs = zip(kept, hold(lax.optimization_barrier((*swapped, s1))[:-1]))
    o0, oy0 = expert(sel, [own], y0, gates, ups, downs, 1)
    o1, oy1 = expert(sel, [after(near, o0)], y1, gates, ups, downs, 1)
    b1 = send(oy1, across)

    far_inner = after(far_inner, o1)
    last_end = send(far_inner, TO_ENDS)
    far = [after(far_end, o1), inner]
    s2, *tables2 = pick_rows(sel, far, experts, cap)
    y2 = send(s2, across)
    q1 = combine(tables1, o1, after(b1, s2))
    r1 = send(q1, FROM_ENDS)
    last = [after(last_end, y2, q1), far_inner]
    s3, *tables3 = pick_rows(sel, last, experts, cap)
    y3 = send(s3, across)
    o2, *oy2 = expert(sel, far, after(y2, s3), gates, ups, downs, HALVES)
    b2 = [send(after(v, y3), across) for v in oy2]
    o3, *oy3 = expert(sel, last, after(y3, o2, r1), gates, ups, downs, HALVES)
    b3 = [send(v, across) for v in oy3]

    part = width // HALVES
    q20 = combine(tables2, o2, after(b2[0], o3), first=0)
    r20 = send(q20, FROM_ENDS)
    q30 = combine(tables3, o3, after(b3[0], q20), first=0)
    r30 = send(q30, FROM_ENDS)
    p20 = add(q20, after(r20, q30))
    r20 = send(p20, INNER)
    q31 = combine(tables3, o3, after(b3[1], p20), first=part)
    r31 = send(q31, FROM_ENDS)
    q21 = combine(tables2, o2, after(b2[1], q31), first=part)
    r21 = send(q21, FROM_ENDS)
    b0 = send(after(oy0, q21), across)
    p30 = add(q30, after(r30, q21))
    r30 = send(p30, INNER)
    p31 = add(q31, after(r31, p30))
    r31 = send(p31, INNER)
    e0 = add(q1[:, :part], after(r30, p31))
    r30 = send(e0, TO_ENDS)
    p21 = add(q21, after(r21, e0))
    r21 = send(p21, INNER)
    e1 = add(q1[:, part:], after(r31, p21))
    r31 = send(e1, TO_ENDS)
    return combine(tables0, o0, b0, extra=([r1], [r20, r21], [r30, r31]), scale=SCALE)


def all_to_all_form(tokens, scores, expert_ids, w_gate, w_up, w_down):
    experts = lax.axis_size("expert")
    tok_rows, width = tokens.shape
    topk = expert_ids.shape[1]
    capacity = capacity_of(tok_rows, topk, experts)
    flat_ids = expert_ids.reshape(-1)
    onehot = (flat_ids[:, None] == jnp.arange(experts, dtype=jnp.int32)[None, :]).astype(jnp.int32)
    position = jnp.sum((jnp.cumsum(onehot, axis=0) - 1) * onehot, axis=1)
    slot = flat_ids * capacity + position
    repeated = jnp.repeat(tokens, topk, axis=0)
    outgoing = jnp.zeros((experts * capacity, width), tokens.dtype).at[slot].set(repeated)
    outgoing = outgoing.reshape(experts, capacity, width)
    doubled = jnp.tile(outgoing, (lax.axis_size("dp"), 1, 1))
    rows = lax.all_to_all(doubled, ("dp", "expert"), split_axis=0, concat_axis=0, tiled=True)
    shape = rows.shape
    flat = rows.reshape(-1, shape[-1])
    gate = dot32(flat, w_gate[0])
    up_value = dot32(flat, w_up[0])
    hidden = (jax.nn.silu(gate) * up_value).astype(jnp.bfloat16)
    partial_value = dot32(hidden, w_down[0]).reshape(shape)
    returned = lax.all_to_all(
        partial_value, ("dp", "expert"), split_axis=0, concat_axis=0, tiled=True
    )
    back = jnp.sum(returned.reshape(-1, experts, capacity, width), axis=0).astype(jnp.bfloat16)
    picked = back.reshape(experts * capacity, width)[slot].reshape(tok_rows, topk, width)
    chosen = jax.nn.sigmoid(jnp.take_along_axis(scores, expert_ids, axis=1))
    weight = chosen / jnp.sum(chosen, axis=1, keepdims=True)
    mixed = SCALE * jnp.sum(weight[:, :, None] * picked.astype(jnp.float32), axis=1)
    return mixed.astype(jnp.bfloat16)


def solution(mesh):
    in_specs = (
        P(("groups", "dp", "expert"), None),
        P(("groups", "dp", "expert"), None),
        P(("groups", "dp", "expert"), None),
        P("expert", None, "dp"),
        P("expert", None, "dp"),
        P("expert", "dp", None),
    )
    out_specs = P(("groups", "dp", "expert"), None)
    short = mesh.shape["expert"] == 8 and mesh.shape["dp"] == 2
    body = four_levels if short else all_to_all_form
    return jax.shard_map(
        body, mesh=mesh, in_specs=in_specs, out_specs=out_specs, check_vma=False
    )
```

```python
import functools

import jax
import jax.numpy as jnp
from jax import lax
from jax.experimental import pallas as pl
from jax.experimental.pallas import tpu as pltpu
from jax.sharding import PartitionSpec as P

LANES = 128
ALIGN = 16
HALVES = 2
VMEM_LIMIT = 24 * 1024 * 1024
SCALE = 2.5
BRIEF = pl.CostEstimate(flops=1, bytes_accessed=1, transcendentals=0)


def up_to(value, step):
    return -(-value // step) * step


def dot32(a, b):
    return jnp.dot(a, b, preferred_element_type=jnp.float32)


def iota(shape, dim):
    return lax.broadcasted_iota(jnp.int32, shape, dim)


def flag(mask):
    return jnp.where(mask, 1.0, 0.0)


def pieces_of(ids_ref, scores_ref):
    topk, rows = ids_ref.shape
    experts = scores_ref.shape[0]
    sig = 1.0 / (1.0 + jnp.exp(-scores_ref[...]))
    ids = [ids_ref[k : k + 1, :] for k in range(topk)]
    row_e = iota((experts, rows), 0)
    chosen = [jnp.sum(jnp.where(i == row_e, sig, 0.0), axis=0, keepdims=True) for i in ids]
    total = sum(chosen[1:], chosen[0])
    row = iota((LANES, rows), 0)
    expert_of_row = lax.rem(row, experts)
    weight = jnp.zeros((LANES, rows), jnp.float32)
    for i, value in zip(ids, chosen):
        weight = weight + jnp.where(i == expert_of_row, value / total, 0.0)
    high = weight.astype(jnp.bfloat16).astype(jnp.float32)
    rest = weight - high
    middle = rest.astype(jnp.bfloat16).astype(jnp.float32)
    low = rest - middle
    pieces = jnp.where(
        row < experts,
        high,
        jnp.where(row < 2 * experts, middle, jnp.where(row < 3 * experts, low, 0.0)),
    )
    return pieces.T


def route(meta, sel_ref, experts, cap):
    rows = meta.shape[0]
    i, j = iota((rows, rows), 0), iota((rows, rows), 1)
    lane = iota((rows, LANES), 1)

    def weight_for(expert):
        hit = (lax.rem(lane, experts) == expert) & (lane < 3 * experts)
        return jnp.sum(jnp.where(hit, meta, 0.0), axis=1, keepdims=True)

    mine, other = weight_for(sel_ref[0]), weight_for(sel_ref[1])
    weights = jnp.where(lane == 0, mine, other)
    named = flag(other > 0.0)
    row_named = jnp.sum(jnp.where(i == j, named, 0.0), axis=0, keepdims=True)
    row_place = jnp.sum(jnp.where(i < j, named, 0.0), axis=0, keepdims=True).astype(jnp.int32)
    place = jnp.sum(jnp.where(j < i, row_named, 0.0), axis=1, keepdims=True).astype(jnp.int32)
    take = flag((iota((cap, rows), 0) == row_place) & (row_named > 0.0))
    back = flag((iota((rows, cap), 1) == place) & (named > 0.0))
    return take.astype(jnp.bfloat16), back.astype(jnp.bfloat16), weights


def open_kernel(sel_ref, ids_ref, scores_ref, tok_ref, packed_ref, y_ref, back_ref, weight_ref):
    width = tok_ref.shape[1]
    pieces = pieces_of(ids_ref, scores_ref)
    packed_ref[:, :width] = tok_ref[...]
    packed_ref[:, width:] = pieces.astype(jnp.bfloat16)
    take, back, weights = route(pieces, sel_ref, scores_ref.shape[0], y_ref.shape[0])
    back_ref[...] = back
    weight_ref[...] = weights
    y_ref[...] = dot32(take, tok_ref[...]).astype(jnp.bfloat16)


def open_block(sel, ids, scores, tokens, cap):
    rows, width = tokens.shape
    return pl.pallas_call(
        open_kernel,
        in_specs=[pl.BlockSpec(memory_space=pltpu.SMEM)]
        + [pl.BlockSpec(memory_space=pltpu.VMEM)] * 3,
        out_shape=[
            jax.ShapeDtypeStruct((rows, width + LANES), jnp.bfloat16),
            jax.ShapeDtypeStruct((cap, width), jnp.bfloat16),
            jax.ShapeDtypeStruct((rows, cap), jnp.bfloat16),
            jax.ShapeDtypeStruct((rows, LANES), jnp.float32),
        ],
        compiler_params=pltpu.CompilerParams(vmem_limit_bytes=VMEM_LIMIT),
        cost_estimate=BRIEF,
        name="open",
    )(sel, ids.T, scores.T, tokens)


def pick_kernel(experts, count, sel_ref, *refs):
    metas, parts, (y_ref, back_ref, weight_ref, held) = refs[:count], refs[count : 2 * count], refs[2 * count :]

    @pl.when(pl.program_id(0) == 0)
    def _():
        meta = metas[0][...].astype(jnp.float32)
        if count == 2:
            meta = jnp.where(sel_ref[2] == 1, meta, metas[1][...].astype(jnp.float32))
        take, back, weights = route(meta, sel_ref, experts, y_ref.shape[0])
        held[...] = take
        back_ref[...] = back
        weight_ref[...] = weights

    for which in range(count):

        @pl.when((sel_ref[2] == 1 - which) | (count == 1))
        def _(which=which):
            y_ref[...] = dot32(held[...], parts[which][...]).astype(jnp.bfloat16)


def pick_rows(sel, parts, experts, cap):
    rows, width = parts[0].shape
    width -= LANES
    block = column_block(width)
    return pl.pallas_call(
        functools.partial(pick_kernel, experts, len(parts)),
        grid=(width // block,),
        in_specs=[pl.BlockSpec(memory_space=pltpu.SMEM)]
        + [pl.BlockSpec((rows, LANES), lambda i: (0, width // LANES))] * len(parts)
        + [pl.BlockSpec((rows, block), lambda i: (0, i))] * len(parts),
        out_specs=[
            pl.BlockSpec((cap, block), lambda i: (0, i)),
            pl.BlockSpec((rows, cap), lambda i: (0, 0)),
            pl.BlockSpec((rows, LANES), lambda i: (0, 0)),
        ],
        out_shape=[
            jax.ShapeDtypeStruct((cap, width), jnp.bfloat16),
            jax.ShapeDtypeStruct((rows, cap), jnp.bfloat16),
            jax.ShapeDtypeStruct((rows, LANES), jnp.float32),
        ],
        scratch_shapes=[pltpu.VMEM((cap, rows), jnp.bfloat16)],
        compiler_params=pltpu.CompilerParams(vmem_limit_bytes=VMEM_LIMIT),
        cost_estimate=BRIEF,
        name="pick",
    )(sel, *parts, *parts)


def hold_kernel(*refs):
    count = len(refs) // 2
    sems = refs[-1]
    copies = [
        pltpu.make_async_copy(refs[k], refs[count + k], sems.at[k]) for k in range(count)
    ]
    for copy in copies:
        copy.start()
    for copy in copies:
        copy.wait()


def hold(weights):
    held = pl.pallas_call(
        hold_kernel,
        in_specs=[pl.BlockSpec(memory_space=pltpu.HBM)] * len(weights),
        out_specs=[pl.BlockSpec(memory_space=pltpu.VMEM)] * len(weights),
        out_shape=[pltpu.VMEM(w.shape, w.dtype) for w in weights],
        scratch_shapes=[pltpu.SemaphoreType.DMA((len(weights),))],
        compiler_params=pltpu.CompilerParams(vmem_limit_bytes=VMEM_LIMIT),
        cost_estimate=BRIEF,
        name="hold",
    )(*weights)
    return [pltpu.with_memory_space_constraint(w, pltpu.VMEM) for w in held]


def expert_kernel(count, halves, sel_ref, *refs):
    parts, y_ref, refs = refs[:count], refs[count], refs[count + 1 :]
    gates, ups, downs, refs = refs[0:2], refs[2:4], refs[4:6], refs[6:]
    out_ref, y_outs, (xs, hidden) = refs[0], refs[1 : 1 + halves], refs[1 + halves :]
    rows, cap = parts[0].shape[0], y_ref.shape[0]
    width, depth = gates[0].shape
    if count == 1:
        xs[:rows, :] = parts[0][:, :width]
    else:
        for which in range(2):

            @pl.when(sel_ref[2] == 1 - which)
            def _(which=which):
                xs[:rows, :] = parts[which][:, :width]

    xs[rows:, :] = y_ref[...]
    block = min(depth, 256)
    for which in range(2):
        for at in range(0, depth, block):
            gate = dot32(xs[...], gates[which][:, at : at + block])
            up = dot32(xs[...], ups[which][:, at : at + block])
            value = gate / (1.0 + jnp.exp(-gate)) * up
            to = which * depth + at
            hidden[:, to : to + block] = value.astype(jnp.bfloat16)
    part = width // halves
    block = column_block(part)
    for at in range(0, width, block):
        columns = slice(at, at + block)
        out = dot32(hidden[:, :depth], downs[0][:, columns])
        out = (out + dot32(hidden[:, depth:], downs[1][:, columns])).astype(jnp.bfloat16)
        out_ref[:, columns] = out[:rows]
        inside = at % part
        y_outs[at // part][:, inside : inside + block] = out[rows:]


def expert(sel, parts, y, gates, ups, downs, halves):
    rows, cap = parts[0].shape[0], y.shape[0]
    width, depth = gates[0].shape
    whole = pl.BlockSpec(memory_space=pltpu.VMEM)
    return pl.pallas_call(
        functools.partial(expert_kernel, len(parts), halves),
        in_specs=[pl.BlockSpec(memory_space=pltpu.SMEM)] + [whole] * (len(parts) + 7),
        out_specs=[whole] * (1 + halves),
        out_shape=[jax.ShapeDtypeStruct((rows, width), jnp.bfloat16)]
        + [jax.ShapeDtypeStruct((cap, width // halves), jnp.bfloat16)] * halves,
        scratch_shapes=[
            pltpu.VMEM((rows + cap, width), jnp.bfloat16),
            pltpu.VMEM((rows + cap, 2 * depth), jnp.bfloat16),
        ],
        compiler_params=pltpu.CompilerParams(vmem_limit_bytes=VMEM_LIMIT),
        cost_estimate=BRIEF,
        name="expert",
    )(sel, *parts, y, *gates, *ups, *downs)


def combine_kernel(scale, back_ref, weight_ref, own_ref, other_ref, *refs):
    weights = weight_ref[...]
    value = weights[:, 0:1] * own_ref[...].astype(jnp.float32)
    value = value + weights[:, 1:2] * dot32(back_ref[...], other_ref[...])
    for ref in refs[:-1]:
        value = value + ref[...].astype(jnp.float32)
    if scale is not None:
        value = value * scale
    refs[-1][...] = value.astype(jnp.bfloat16)


def into_kernel(scale, *refs):
    combine_kernel(scale, *refs[:-2], refs[-1])


def combine(tables, own, other, extra=(), first=0, count=None, scale=None, into=None):
    rows, full = own.shape
    cap, width = other.shape
    count = count or width
    block = column_block(count)
    offset = first // block

    def columns(array):
        shift = offset if array.shape[1] == full else 0
        return pl.BlockSpec((array.shape[0], block), lambda i: (0, i + shift))

    whole = full if scale is not None else count
    shift = offset if scale is not None else 0
    operands = [*tables, own, other, *extra]
    in_specs = [
        pl.BlockSpec((rows, cap), lambda i: (0, 0)),
        pl.BlockSpec((rows, LANES), lambda i: (0, 0)),
    ] + [columns(array) for array in operands[2:]]
    body = combine_kernel
    aliases = {}
    if into is not None:
        aliases = {len(operands): 0}
        operands.append(into)
        in_specs.append(pl.BlockSpec(memory_space=pl.ANY))
        body = into_kernel
    return pl.pallas_call(
        functools.partial(body, scale),
        grid=(count // block,),
        in_specs=in_specs,
        out_specs=pl.BlockSpec((rows, block), lambda i: (0, i + shift)),
        out_shape=jax.ShapeDtypeStruct((rows, whole), jnp.bfloat16),
        input_output_aliases=aliases,
        compiler_params=pltpu.CompilerParams(vmem_limit_bytes=VMEM_LIMIT),
        cost_estimate=BRIEF,
        name="combine",
    )(*operands)


def column_block(width):
    return 896 if width % 896 == 0 else width


def capacity_of(tok_rows, topk, experts):
    return min(tok_rows, max(2, 5 * tok_rows * topk // (2 * experts)))


def on_levels(pairs):
    return [(2 * a + y, 2 * b + y) for a, b in pairs for y in range(2)]


OUTER = on_levels([(0, 1), (1, 0), (2, 3), (3, 2)])
INNER = on_levels([(1, 2), (2, 1)])
TO_ENDS = on_levels([(1, 0), (2, 3)])
FROM_ENDS = on_levels([(0, 1), (3, 2)])


def after(value, *others):
    return lax.optimization_barrier((value, *others))[0]


def add(a, b):
    return (a.astype(jnp.float32) + b.astype(jnp.float32)).astype(jnp.bfloat16)


def four_levels(tokens, scores, expert_ids, w_gate, w_up, w_down):
    experts = lax.axis_size("expert")
    tok_rows, width = tokens.shape
    topk = expert_ids.shape[1]
    cap = min(tok_rows, up_to(capacity_of(tok_rows, topk, experts), ALIGN))
    me = lax.axis_index("expert")
    level = me // 2
    end = ((level == 0) | (level == 3)).astype(jnp.int32)
    sel = jnp.stack([me, me ^ 1, end]).astype(jnp.int32)
    across = [(i, i ^ 1) for i in range(experts)]

    def send(value, pairs):
        return lax.ppermute(value, "expert", pairs)

    def swap(value):
        return lax.ppermute(value, "dp", [(0, 1), (1, 0)])

    swapped = [swap(w[0]) for w in (w_gate, w_up, w_down)]
    own, s0, *tables0 = open_block(sel, expert_ids, scores, tokens, cap)
    near = send(own, OUTER)
    inner = send(own, INNER)
    y0 = send(after(s0, swapped[0]), across)

    kept = hold(lax.optimization_barrier((w_gate[0], w_up[0], w_down[0], own))[:-1])
    near = after(near, y0, kept[0])
    far_inner = send(near, INNER)
    far_end = send(inner, TO_ENDS)
    s1, *tables1 = pick_rows(sel, [near], experts, cap)
    y1 = send(s1, across)
    gates, ups, downs = zip(kept, hold(lax.optimization_barrier((*swapped, s1))[:-1]))
    o0, oy0 = expert(sel, [own], y0, gates, ups, downs, 1)
    o1, oy1 = expert(sel, [after(near, o0)], y1, gates, ups, downs, 1)
    b1 = send(oy1, across)

    far_inner = after(far_inner, o1)
    last_end = send(far_inner, TO_ENDS)
    far = [after(far_end, o1), inner]
    s2, *tables2 = pick_rows(sel, far, experts, cap)
    y2 = send(s2, across)
    q1 = combine(tables1, o1, after(b1, s2))
    r1 = send(q1, FROM_ENDS)
    last = [after(last_end, y2, q1), far_inner]
    s3, *tables3 = pick_rows(sel, last, experts, cap)
    y3 = send(s3, across)
    o2, *oy2 = expert(sel, far, after(y2, s3), gates, ups, downs, HALVES)
    b2 = [send(after(v, y3), across) for v in oy2]
    o3, *oy3 = expert(sel, last, after(y3, o2, r1), gates, ups, downs, HALVES)
    b3 = [send(v, across) for v in oy3]

    part = width // HALVES
    q20 = combine(tables2, o2, after(b2[0], o3), first=0)
    r20 = send(q20, FROM_ENDS)
    q30 = combine(tables3, o3, after(b3[0], q20), first=0)
    r30 = send(q30, FROM_ENDS)
    p20 = add(q20, after(r20, q30))
    r20 = send(p20, INNER)
    q31 = combine(tables3, o3, after(b3[1], p20), first=part)
    r31 = send(q31, FROM_ENDS)
    q21 = combine(tables2, o2, after(b2[1], q31), first=part)
    r21 = send(q21, FROM_ENDS)
    b0 = send(after(oy0, q21), across)
    p30 = add(q30, after(r30, q21))
    r30 = send(p30, INNER)
    p31 = add(q31, after(r31, p30))
    r31 = send(p31, INNER)
    e0 = add(q1[:, :part], after(r30, p31))
    r30 = send(e0, TO_ENDS)
    p21 = add(q21, after(r21, e0))
    r21 = send(p21, INNER)
    e1 = add(q1[:, part:], after(r31, p21))
    r31 = send(e1, TO_ENDS)
    mixed = combine(tables0, o0, b0, (r1, r20, r30), first=0, count=part, scale=SCALE)
    return combine(
        tables0, o0, b0, (r1, r21, after(r31, mixed)), first=part, count=part, scale=SCALE, into=mixed
    )


def all_to_all_form(tokens, scores, expert_ids, w_gate, w_up, w_down):
    experts = lax.axis_size("expert")
    tok_rows, width = tokens.shape
    topk = expert_ids.shape[1]
    capacity = capacity_of(tok_rows, topk, experts)
    flat_ids = expert_ids.reshape(-1)
    onehot = (flat_ids[:, None] == jnp.arange(experts, dtype=jnp.int32)[None, :]).astype(jnp.int32)
    position = jnp.sum((jnp.cumsum(onehot, axis=0) - 1) * onehot, axis=1)
    slot = flat_ids * capacity + position
    repeated = jnp.repeat(tokens, topk, axis=0)
    outgoing = jnp.zeros((experts * capacity, width), tokens.dtype).at[slot].set(repeated)
    outgoing = outgoing.reshape(experts, capacity, width)
    doubled = jnp.tile(outgoing, (lax.axis_size("dp"), 1, 1))
    rows = lax.all_to_all(doubled, ("dp", "expert"), split_axis=0, concat_axis=0, tiled=True)
    shape = rows.shape
    flat = rows.reshape(-1, shape[-1])
    gate = dot32(flat, w_gate[0])
    up_value = dot32(flat, w_up[0])
    hidden = (jax.nn.silu(gate) * up_value).astype(jnp.bfloat16)
    partial_value = dot32(hidden, w_down[0]).reshape(shape)
    returned = lax.all_to_all(
        partial_value, ("dp", "expert"), split_axis=0, concat_axis=0, tiled=True
    )
    back = jnp.sum(returned.reshape(-1, experts, capacity, width), axis=0).astype(jnp.bfloat16)
    picked = back.reshape(experts * capacity, width)[slot].reshape(tok_rows, topk, width)
    chosen = jax.nn.sigmoid(jnp.take_along_axis(scores, expert_ids, axis=1))
    weight = chosen / jnp.sum(chosen, axis=1, keepdims=True)
    mixed = SCALE * jnp.sum(weight[:, :, None] * picked.astype(jnp.float32), axis=1)
    return mixed.astype(jnp.bfloat16)


def solution(mesh):
    in_specs = (
        P(("groups", "dp", "expert"), None),
        P(("groups", "dp", "expert"), None),
        P(("groups", "dp", "expert"), None),
        P("expert", None, "dp"),
        P("expert", None, "dp"),
        P("expert", "dp", None),
    )
    out_specs = P(("groups", "dp", "expert"), None)
    short = mesh.shape["expert"] == 8 and mesh.shape["dp"] == 2
    body = four_levels if short else all_to_all_form
    return jax.shard_map(
        body, mesh=mesh, in_specs=in_specs, out_specs=out_specs, check_vma=False
    )
```
